32 devices in a mesh: dp: 4 (over z), ctx: 8 (over y, x, core).
Axes of the slice: x: 2, y: 2, z: 4, core: 2. Of those that a mesh axis runs over, the one named last changes fastest.
Arguments:
- events: bfloat16 [16384, 1024], P(('dp', 'ctx')), parts along dimension 0, may hold values from -48 to 48
- destination: int32 [16384], P(('dp', 'ctx')), parts along dimension 0, may hold values from 0 to 4095, as said below
- segment: int32 [16384], P(('dp', 'ctx')), parts along dimension 0, may hold values from 0 to 3, never falling along the last dimension, each value on 1 to 3072 neighbouring positions
- w_query: bfloat16 [1024, 1024], replicated, may hold values from -0.375 to 0.375
- key_weight: bfloat16 [1024, 256], replicated, may hold values from -0.1875 to 0.1875
- value_weight: bfloat16 [1024, 256], replicated, may hold values from -0.75 to 0.75
Outputs:
- attended: bfloat16 [16384, 1024], P(('dp', 'ctx')), parts along dimension 0
The draws below stay inside these ranges and needn't reach their ends.
There are 4 independent parts, one for each index of `dp`. The reference program is written for one: setup_inputs(seed, part) draws one part's arguments, and reference() takes and returns one part's arrays. A program takes and returns all parts, laid end to end along the dimension named above; an argument that names none is the same for every part. Nothing has to cross between parts.
Inputs may be any that keep to these rules, and one draw needn't show every extreme that they name: destination is a permutation that moves stored events in aligned blocks of 64 rows, keeping their order inside a block; the 8 blocks of one device land on 8 different devices' ranges of 512 packed positions, so at most 64 rows of one device reach one device's range.
All inputs are finite; a program needn't handle non-finite values.
Results may differ from the reference program's by a relative error of at most 0.0045.
The reference program's roundings to bfloat16 on the way count: a program that leaves them out, or rounds other values in their place, can miss the bound.
Values may be sent and summed in bfloat16 or wider, within the bound.
A program may use at most 64 MiB of HBM per device.

```python
import math
import jax
import jax.numpy as jnp
import numpy as np
from jax import lax

MODEL_WIDTH = 1024
QUERY_HEADS = 8
KEY_VALUE_HEADS = 2
HEAD_SIZE = 128
TOK_DEV = 512
BLOCKS = 8
BLK = 64
SEQ = 4096


def draw_events(key, part):
    first = jax.random.fold_in(key, 0)
    value_rows = jnp.clip(jax.random.normal(first, (SEQ, MODEL_WIDTH), jnp.float32), -6.0, 6.0)
    return value_rows.astype(jnp.bfloat16)


def draw_destination(key, part):
    ndevices = SEQ // TOK_DEV
    first, second = jax.random.split(key)
    offsets = jax.random.permutation(first, ndevices)[:BLOCKS]
    slots = jax.vmap(lambda dev: jax.random.permutation(jax.random.fold_in(second, dev), BLOCKS))(jnp.arange(ndevices))
    token_rows = jnp.arange(SEQ, dtype=jnp.int32)
    source = token_rows // TOK_DEV
    block = token_rows % TOK_DEV // BLK
    inner = token_rows % BLK
    target = (source + offsets[block]) % ndevices
    place = slots[target, block]
    return (target * TOK_DEV + place * BLK + inner).astype(jnp.int32)


def length_profile(number_of, total, bound, lean):
    loads = [(1 << 20) // math.isqrt(rank ** lean) + 1 for rank in range(2, number_of + 1)]
    spare, given = total - bound - (number_of - 1), [1] * (number_of - 1)
    while spare > 0:
        free = [i for i in range(number_of - 1) if given[i] < bound]
        whole, left = sum([loads[i] for i in free]), spare
        for i in free:
            extra = min(bound - given[i], max(1, left * loads[i] // whole), spare)
            given[i] = given[i] + extra
            spare = spare - extra
    return np.array([bound] + given)


def ragged(own_key, count, total, bound, skew):
    if count == 2:
        one = jax.random.randint(own_key, (), max(1, total - bound), min(bound, total - 1) + 1)
        return jnp.stack([one, total - one])
    lengths = jnp.asarray(length_profile(count, total, bound, skew), jnp.int32)
    couples = (count - 1) // 2
    donor, sink = lengths[1:1 + 2 * couples:2], lengths[2:2 + 2 * couples:2]
    margin = jnp.minimum(donor - 1, bound - sink)
    moved = jax.random.randint(jax.random.fold_in(own_key, 1), (couples,), 0, 1 << 20) % (margin + 1)
    lengths = lengths.at[1:1 + 2 * couples:2].set(donor - moved).at[2:2 + 2 * couples:2].set(sink + moved)
    return lengths[jax.random.permutation(jax.random.fold_in(own_key, 2), count)]


def bell_draw(key, extent, deviation, reach, held_as=jnp.bfloat16):
    result = jax.random.normal(key, extent, jnp.float32) * deviation
    return jnp.minimum(jnp.maximum(result, -reach), reach).astype(held_as)


def setup_inputs(seed: int = 0, part: int = 0) -> dict:
    key_list = jax.random.split(jax.random.key(seed), 7)
    part_keys = jax.random.split(jax.random.fold_in(key_list[6], part), 7)
    events = draw_events(jax.random.fold_in(jax.random.fold_in(key_list[6], part), 71), part)
    destination = draw_destination(jax.random.fold_in(jax.random.fold_in(key_list[6], part), 71), part)
    segment = jnp.searchsorted(jnp.cumsum(ragged(part_keys[2], 4, SEQ, 3 * SEQ // 4, 0)), jnp.arange(SEQ), side="right").astype(jnp.int32)
    w_query = bell_draw(key_list[3], (MODEL_WIDTH, QUERY_HEADS * HEAD_SIZE), (MODEL_WIDTH // 4) ** -0.5, 0.375)
    key_weight = bell_draw(key_list[4], (MODEL_WIDTH, KEY_VALUE_HEADS * HEAD_SIZE), MODEL_WIDTH ** -0.5, 0.1875)
    value_weight = bell_draw(key_list[5], (MODEL_WIDTH, KEY_VALUE_HEADS * HEAD_SIZE), (MODEL_WIDTH // 16) ** -0.5, 0.75)
    return {"events": events, "destination": destination, "segment": segment, "w_query": w_query, "key_weight": key_weight, "value_weight": value_weight}


def reference(events, destination, segment, w_query, key_weight, value_weight):
    history_length = events.shape[0]
    packed = jnp.zeros_like(events).at[destination].set(events)
    query_rows = jnp.dot(packed, w_query, preferred_element_type=jnp.float32).astype(jnp.bfloat16)
    key_rows = jnp.dot(packed, key_weight, preferred_element_type=jnp.float32).astype(jnp.bfloat16)
    value_rows = jnp.dot(packed, value_weight, preferred_element_type=jnp.float32).astype(jnp.bfloat16)
    group_size = QUERY_HEADS // KEY_VALUE_HEADS
    score_scale = 1.0 / math.sqrt(HEAD_SIZE)
    gathered_keys = key_rows.astype(jnp.float32).reshape(history_length, KEY_VALUE_HEADS, HEAD_SIZE)
    gathered_values = value_rows.astype(jnp.float32).reshape(history_length, KEY_VALUE_HEADS, HEAD_SIZE)
    positions = jnp.arange(history_length, dtype=jnp.int32)
    token_span = min(512, history_length)

    def one_block(block):
        start = (block * token_span).astype(jnp.int32)
        token_rows = lax.dynamic_slice_in_dim(query_rows, start, token_span, 0).astype(jnp.float32)
        token_rows = token_rows.reshape(token_span, KEY_VALUE_HEADS, group_size, HEAD_SIZE)
        row_pos = start + jnp.arange(token_span, dtype=jnp.int32)
        row_seg = lax.dynamic_slice_in_dim(segment, start, token_span, 0)
        logit_scores = jnp.einsum('qxli,oxi->xlqo', token_rows, gathered_keys) * score_scale
        allowed = (segment[None, :] == row_seg[:, None]) & (positions[None, :] <= row_pos[:, None])
        logit_scores = jnp.where(allowed, logit_scores, -jnp.inf)
        rowmax = lax.optimization_barrier(jnp.max(logit_scores, axis=-1))
        expd = jnp.where(allowed, jnp.exp(logit_scores - rowmax[..., None]), 0.0)
        total_tokens = lax.optimization_barrier(jnp.sum(expd, axis=-1))
        softmax_weights = lax.optimization_barrier(expd.astype(jnp.bfloat16)).astype(jnp.float32)
        mixed_output = jnp.einsum('qlwc,cqh->qlwh', softmax_weights, gathered_values) / total_tokens[..., None]
        return mixed_output.transpose(2, 0, 1, 3).reshape(token_span, QUERY_HEADS * HEAD_SIZE).astype(jnp.bfloat16)
    blocks = lax.map(one_block, jnp.arange(history_length // token_span, dtype=jnp.int32))
    return blocks.reshape(history_length, QUERY_HEADS * HEAD_SIZE)
```

```python
import functools
import math

import jax
import jax.numpy as jnp
from jax import lax
from jax.experimental import pallas as pl
from jax.experimental.pallas import tpu as pltpu
from jax.sharding import PartitionSpec as P

QUERY_HEADS = 8
KEY_VALUE_HEADS = 2
HEAD_SIZE = 128
GROUP = QUERY_HEADS // KEY_VALUE_HEADS
BLOCKS = 8
SEGMENTS = 4
LANES = 128

NEGATIVE_FILL = -1e30
SCALE = math.log2(math.e) / math.sqrt(HEAD_SIZE)
NT = (((1,), (1,)), ((), ()))


def fused_kernel(
    dest_ref, seg_ref, events_hbm, wq_hbm, wk_hbm, wv_hbm, out_ref,
    events, wq, wk, wv, rows_sorted, info_send, info, kv_send, kv, q_local, q_all,
    pair_pos, pair_start, key_pos, values_t, best, accum, o_send, o_recv,
    load_sem, info_ssem, info_rsem, kv_ssem, kv_rsem, q_sem, o_ssem, o_rsem,
):
    tokens = events.shape[0]
    n = BLOCKS
    blk = tokens // n
    wide = GROUP * HEAD_SIZE
    me = lax.axis_index("ctx")
    core = me % 2
    chip = me // 2
    sibling = chip * 2 + 1 - core
    f32 = jnp.float32

    loads = [
        pltpu.make_async_copy(src, dst, load_sem.at[k])
        for k, (src, dst) in enumerate(
            ((events_hbm, events), (wk_hbm, wk), (wv_hbm, wv), (wq_hbm, wq))
        )
    ]
    for load in loads:
        load.start()

    barrier = pltpu.get_barrier_semaphore()
    for d in range(1, n):
        pl.semaphore_signal(
            barrier, inc=1, device_id={"ctx": (me + d) % n}, device_id_type=pl.DeviceIdType.MESH
        )

    dest = dest_ref[...]
    target = jnp.zeros_like(dest)
    for j in range(1, n):
        target = target + (dest >= j * tokens).astype(jnp.int32)
    row_of = lax.broadcasted_iota(jnp.int32, (n, tokens), 0)
    base = jnp.min(
        jnp.where(jnp.broadcast_to(target, (n, tokens)) == row_of, dest.astype(f32), 1e9),
        axis=1, keepdims=True,
    )
    below = jnp.sum(
        jnp.where(jnp.broadcast_to(seg_ref[...], (n, tokens)) < row_of, 1.0, 0.0),
        axis=1, keepdims=True,
    )
    info_send[0:n, :] = jnp.broadcast_to(base, (n, LANES))
    info_send[n : 2 * n, :] = jnp.broadcast_to(below, (n, LANES))
    info[me] = info_send[...]

    lane = lax.broadcasted_iota(jnp.int32, (1, tokens), 1)
    rank = target * blk + lane % blk
    place = lax.broadcasted_iota(jnp.int32, (tokens, tokens), 0) == rank
    order = jnp.where(place, 1.0, 0.0).astype(jnp.bfloat16)

    pl.semaphore_wait(barrier, n - 1)

    def info_copy(d):
        peer = (me + d) % n
        return pltpu.make_async_remote_copy(
            info_send, info.at[me], info_ssem.at[d], info_rsem.at[me],
            device_id={"ctx": peer}, device_id_type=pl.DeviceIdType.MESH,
        )

    for d in range(1, n):
        info_copy(d).start()

    loads[0].wait()
    rows_sorted[...] = jnp.dot(order, events[...], preferred_element_type=f32).astype(jnp.bfloat16)
    loads[1].wait()
    loads[2].wait()
    keys = jnp.dot(rows_sorted[...], wk[...], preferred_element_type=f32).astype(jnp.bfloat16)
    values = jnp.dot(rows_sorted[...], wv[...], preferred_element_type=f32).astype(jnp.bfloat16)
    for h in range(KEY_VALUE_HEADS):
        cols = slice(h * HEAD_SIZE, (h + 1) * HEAD_SIZE)
        kv_send[h, :, :, 0:HEAD_SIZE] = keys[:, cols].reshape(n, blk, HEAD_SIZE)
        kv_send[h, :, :, HEAD_SIZE:] = values[:, cols].reshape(n, blk, HEAD_SIZE)

    def kv_copy(j, d, c):
        to_chip = (chip + d) % (n // 2)
        return pltpu.make_async_remote_copy(
            kv_send.at[c, j], kv.at[j, me], kv_ssem.at[j, 2 * d + c], kv_rsem.at[j, me],
            device_id={"ctx": to_chip * 2 + c}, device_id_type=pl.DeviceIdType.MESH,
        )

    def sibling_kv(j):
        return pltpu.make_async_remote_copy(
            kv_send.at[1 - core, j], kv.at[j, me], kv_ssem.at[j, 0], kv_rsem.at[j, me],
            device_id={"ctx": sibling}, device_id_type=pl.DeviceIdType.MESH,
        )

    @pl.loop(0, n)
    def _(j):
        for d in range(1, n // 2):
            for c in range(2):
                kv_copy(j, d, c).start()
        sibling_kv(j).start()
        kv[j, me] = kv_send[core, j]

    loads[3].wait()
    for h in range(KEY_VALUE_HEADS):
        query = jnp.dot(
            rows_sorted[...], wq[:, h * wide : (h + 1) * wide], preferred_element_type=f32
        ).astype(jnp.bfloat16)
        for e in range(GROUP):
            q_local[h, :, e] = query[:, e * HEAD_SIZE : (e + 1) * HEAD_SIZE].reshape(
                n, blk, HEAD_SIZE
            )
    q_copy = pltpu.make_async_remote_copy(
        q_local.at[1 - core], q_all.at[core], q_sem.at[0], q_sem.at[1],
        device_id={"ctx": sibling}, device_id_type=pl.DeviceIdType.MESH,
    )
    q_copy.start()
    q_all[core] = q_local[core]

    best[...] = jnp.full(best.shape, NEGATIVE_FILL, f32)
    accum[...] = jnp.zeros(accum.shape, f32)
    values_t[HEAD_SIZE:, :] = jnp.ones((values_t.shape[0] - HEAD_SIZE, tokens), jnp.bfloat16)

    for d in range(1, n):
        source = (me + d) % n
        pltpu.make_async_remote_copy(
            info_send, info.at[source], info_ssem.at[d], info_rsem.at[source],
            device_id={"ctx": source}, device_id_type=pl.DeviceIdType.MESH,
        ).wait_recv()

    counts = jnp.sum(info[:, n : 2 * n, :], axis=0)
    pair = lax.broadcasted_iota(jnp.int32, (n, 2 * blk), 1)
    for c in range(n // 2):
        where = jnp.where(pair < blk, info[2 * c, 0:n, :], info[2 * c + 1, 0:n, :])
        pair_pos[c] = where + (pair % blk).astype(f32)
    mine = pair_pos[chip]
    start = jnp.zeros_like(mine)
    for s in range(1, SEGMENTS):
        edge = jnp.broadcast_to(counts[s : s + 1, :], mine.shape)
        start = jnp.maximum(start, jnp.where(mine >= edge, edge, 0.0))
    pair_start[...] = start

    q_copy.wait_recv()

    def o_copy(i):
        return pltpu.make_async_remote_copy(
            o_send.at[i], o_recv.at[core, chip], o_ssem.at[i], o_rsem.at[me],
            device_id={"ctx": i}, device_id_type=pl.DeviceIdType.MESH,
        )

    @pl.loop(0, n)
    def _(j):
        for d in range(1, n):
            source = (me + d) % n
            pltpu.make_async_remote_copy(
                kv_send.at[0, j], kv.at[j, source], kv_ssem.at[j, 0], kv_rsem.at[j, source],
                device_id={"ctx": source}, device_id_type=pl.DeviceIdType.MESH,
            ).wait_recv()
        block = kv[j].reshape(tokens, 2 * HEAD_SIZE)
        values_t[0:HEAD_SIZE, :] = block[:, HEAD_SIZE:].astype(f32).T.astype(jnp.bfloat16)
        for s in range(n):
            key_pos[s * blk : (s + 1) * blk, :] = info[s, pl.ds(j, 1), :] + lax.broadcasted_iota(
                jnp.int32, (blk, LANES), 0
            ).astype(f32)
        key_tile = block[:, 0:HEAD_SIZE]

        @pl.loop(j, n)
        def _(i):
            here = pair_pos[chip, pl.ds(i, 1), :]
            start = pair_start[pl.ds(i, 1), :]
            at = key_pos[...]
            bias = jnp.where((at >= start) & (at <= here), 0.0, NEGATIVE_FILL)
            bias = jnp.concatenate([bias, bias], axis=1)
            for half in range(2):
                cols = slice(half * 4 * blk, (half + 1) * 4 * blk)
                query = jnp.concatenate(
                    [
                        q_all[c, i, 2 * half + e]
                        for e in range(2)
                        for c in range(2)
                    ],
                    axis=0,
                )
                scores = lax.dot_general(key_tile, query, NT, preferred_element_type=f32) + bias
                old = best[i, :, cols]
                fresh = jnp.maximum(old, jnp.max(scores, axis=0, keepdims=True))
                weights = jnp.exp2((scores - fresh) * SCALE).astype(jnp.bfloat16)
                best[i, :, cols] = fresh
                accum[i, :, cols] = accum[i, :, cols] * jnp.exp2((old - fresh) * SCALE) + jnp.dot(
                    values_t[...], weights, preferred_element_type=f32
                )

            @pl.when(i == j)
            def _():
                for e in range(GROUP):
                    cols = slice(e * 2 * blk, (e + 1) * 2 * blk)
                    mixed = accum[i, 0:HEAD_SIZE, cols] / accum[i, HEAD_SIZE : HEAD_SIZE + 1, cols]
                    o_send[i, :, e * HEAD_SIZE : (e + 1) * HEAD_SIZE] = mixed.T.astype(jnp.bfloat16)

                @pl.when(i != me)
                def _():
                    o_copy(i).start()

                @pl.when(i == me)
                def _():
                    o_recv[core, chip] = o_send[i]

    origin = (me * tokens).astype(f32)
    into = jnp.concatenate([pair_pos[c, pl.ds(me, 1), :] for c in range(n // 2)], axis=1) - origin
    row = lax.broadcasted_iota(jnp.int32, (tokens, tokens), 0).astype(f32)
    order = jnp.where(row == into, 1.0, 0.0).astype(jnp.bfloat16)
    for d in range(1, n):
        source = (me + d) % n
        pltpu.make_async_remote_copy(
            o_send.at[0], o_recv.at[source % 2, source // 2], o_ssem.at[0], o_rsem.at[source],
            device_id={"ctx": source}, device_id_type=pl.DeviceIdType.MESH,
        ).wait_recv()
    for c in range(2):
        got = o_recv[c].reshape(tokens, wide)
        out_ref[:, c * wide : (c + 1) * wide] = jnp.dot(
            order, got, preferred_element_type=f32
        ).astype(jnp.bfloat16)

    for d in range(1, n):
        info_copy(d).wait_send()
    q_copy.wait_send()

    @pl.loop(0, n)
    def _(j):
        for d in range(1, n // 2):
            for c in range(2):
                kv_copy(j, d, c).wait_send()
        sibling_kv(j).wait_send()

        @pl.when(j != me)
        def _():
            o_copy(j).wait_send()


def on_device_fused(events, destination, segment, w_query, key_weight, value_weight):
    tokens, width = events.shape
    n = BLOCKS
    blk = tokens // n
    wide = GROUP * HEAD_SIZE
    bf16, f32 = jnp.bfloat16, jnp.float32
    vmem = pl.BlockSpec(memory_space=pltpu.VMEM)
    hbm = pl.BlockSpec(memory_space=pl.ANY)
    dma = pltpu.SemaphoreType.DMA
    return pl.pallas_call(
        fused_kernel,
        out_shape=jax.ShapeDtypeStruct((tokens, QUERY_HEADS * HEAD_SIZE), bf16),
        in_specs=[vmem, vmem, hbm, hbm, hbm, hbm],
        out_specs=vmem,
        scratch_shapes=[
            pltpu.VMEM((tokens, width), bf16),
            pltpu.VMEM(w_query.shape, bf16),
            pltpu.VMEM(key_weight.shape, bf16),
            pltpu.VMEM(value_weight.shape, bf16),
            pltpu.VMEM((tokens, width), bf16),
            pltpu.VMEM((2 * n, LANES), f32),
            pltpu.VMEM((n, 2 * n, LANES), f32),
            pltpu.VMEM((KEY_VALUE_HEADS, n, blk, 2 * HEAD_SIZE), bf16),
            pltpu.VMEM((n, n, blk, 2 * HEAD_SIZE), bf16),
            pltpu.VMEM((KEY_VALUE_HEADS, n, GROUP, blk, HEAD_SIZE), bf16),
            pltpu.VMEM((2, n, GROUP, blk, HEAD_SIZE), bf16),
            pltpu.VMEM((n // 2, n, LANES), f32),
            pltpu.VMEM((n, LANES), f32),
            pltpu.VMEM((tokens, LANES), f32),
            pltpu.VMEM((HEAD_SIZE + 16, tokens), bf16),
            pltpu.VMEM((n, 1, GROUP * 2 * blk), f32),
            pltpu.VMEM((n, HEAD_SIZE + 16, GROUP * 2 * blk), f32),
            pltpu.VMEM((n, 2 * blk, wide), bf16),
            pltpu.VMEM((2, n // 2, 2 * blk, wide), bf16),
            dma((4,)),
            dma((n,)),
            dma((n,)),
            dma((n, n)),
            dma((n, n)),
            dma((2,)),
            dma((n,)),
            dma((n,)),
        ],
        compiler_params=pltpu.CompilerParams(
            collective_id=0, has_side_effects=True, vmem_limit_bytes=56 * 1024 * 1024
        ),
    )(destination.reshape(1, tokens), segment.reshape(1, tokens), events, w_query, key_weight, value_weight)


def on_device_general(events, destination, segment, w_query, key_weight, value_weight):
    token_count = events.shape[0]
    width = events.shape[1]
    ndevices = lax.axis_size("ctx")
    myself = lax.axis_index("ctx")
    group_size = QUERY_HEADS // KEY_VALUE_HEADS
    score_scale = 1.0 / math.sqrt(HEAD_SIZE)
    lanes = jnp.arange(ndevices, dtype=jnp.int32)
    local_rows = jnp.arange(token_count, dtype=jnp.int32)
    target = destination // token_count
    place = destination % token_count
    bucket = token_count // BLOCKS
    own_position = myself * token_count + local_rows
    onehot = (target[:, None] == lanes[None, :]).astype(jnp.int32)
    earlier = (local_rows[None, :] < local_rows[:, None]).astype(jnp.float32)
    before = jnp.dot(earlier, onehot.astype(jnp.float32)).astype(jnp.int32)
    slot = jnp.sum(before * onehot, axis=1)
    index = target * bucket + slot
    send_rows = (
        jnp.zeros((ndevices * bucket, width), events.dtype)
        .at[index]
        .set(events)
        .reshape(ndevices, bucket, width)
    )
    send_place = (
        jnp.full((ndevices * bucket,), token_count, jnp.int32)
        .at[index]
        .set(place)
        .reshape(ndevices, bucket)
    )
    got_rows, got_place = (
        lax.all_to_all(send_rows, "ctx", split_axis=0, concat_axis=0, tiled=True),
        lax.all_to_all(send_place, "ctx", split_axis=0, concat_axis=0, tiled=True),
    )
    packed = (
        jnp.zeros((token_count, width), events.dtype)
        .at[got_place.reshape(-1)]
        .set(got_rows.reshape(-1, width), mode="drop")
    )
    query_rows = jnp.dot(packed, w_query, preferred_element_type=jnp.float32).astype(jnp.bfloat16)
    key_rows = jnp.dot(packed, key_weight, preferred_element_type=jnp.float32).astype(jnp.bfloat16)
    value_rows = jnp.dot(packed, value_weight, preferred_element_type=jnp.float32).astype(
        jnp.bfloat16
    )
    query_head_rows = query_rows.reshape(token_count, KEY_VALUE_HEADS, group_size, HEAD_SIZE)
    query_seg = segment.astype(jnp.float32)
    seg_sent = segment.astype(jnp.bfloat16)
    start_state = (
        jnp.full((KEY_VALUE_HEADS, group_size, token_count), NEGATIVE_FILL, jnp.float32),
        jnp.zeros((KEY_VALUE_HEADS, group_size, token_count), jnp.float32),
        jnp.zeros((KEY_VALUE_HEADS, group_size, token_count, HEAD_SIZE), jnp.float32),
    )
    carry = start_state
    key_portion = lax.all_gather(key_rows, "ctx", axis=0, tiled=True)
    value_portion = lax.all_gather(value_rows, "ctx", axis=0, tiled=True)
    seg_piece = lax.all_gather(seg_sent, "ctx", axis=0, tiled=True)
    token_rows = key_portion.shape[0]
    block_step = 512
    event_count = token_rows // block_step
    key_block_list = key_portion.reshape(event_count, block_step, KEY_VALUE_HEADS, HEAD_SIZE)
    value_block_list = value_portion.reshape(event_count, block_step, KEY_VALUE_HEADS, HEAD_SIZE)
    seg_blocks = seg_piece.astype(jnp.float32).reshape(event_count, block_step)
    offsets = jnp.arange(event_count, dtype=jnp.int32) * block_step

    def one_block(state, inputs):
        key_tile_rows, value_block, seg_block, offset = inputs
        key_pos = offset + jnp.arange(block_step, dtype=jnp.int32)
        allowed = (seg_block[None, :] == query_seg[:, None]) & (
            key_pos[None, :] <= own_position[:, None]
        )
        best, total_tokens, accum = state
        logit_scores = (
            jnp.einsum(
                "qxli,oxi->xlqo", query_head_rows, key_tile_rows, preferred_element_type=jnp.float32
            )
            * score_scale
        )
        logit_scores = jnp.where(allowed, logit_scores, NEGATIVE_FILL)
        fresh = jnp.maximum(best, jnp.max(logit_scores, axis=-1))
        softmax_weights = jnp.where(allowed, jnp.exp(logit_scores - fresh[..., None]), 0.0)
        shrink = jnp.exp(best - fresh)
        total_tokens = total_tokens * shrink + jnp.sum(softmax_weights, axis=-1)
        accum = accum * shrink[..., None] + jnp.einsum(
            "qlwc,cqh->qlwh",
            softmax_weights.astype(jnp.bfloat16),
            value_block,
            preferred_element_type=jnp.float32,
        )
        state = (fresh, total_tokens, accum)
        return (state, None)

    carry, _ = lax.scan(one_block, carry, (key_block_list, value_block_list, seg_blocks, offsets))
    best, total_tokens, accum = carry
    result = (
        (accum / total_tokens[..., None])
        .transpose(2, 0, 1, 3)
        .reshape(token_count, QUERY_HEADS * HEAD_SIZE)
        .astype(jnp.bfloat16)
    )
    return result


def solution(mesh):
    def on_device(events, *rest):
        fits = mesh.shape["ctx"] == BLOCKS and events.shape[0] == BLOCKS * LANES // 2
        return (on_device_fused if fits else on_device_general)(events, *rest)

    return jax.shard_map(
        on_device,
        mesh=mesh,
        in_specs=(P(("dp", "ctx"), None), P(("dp", "ctx")), P(("dp", "ctx")), P(), P(), P()),
        out_specs=P(("dp", "ctx"), None),
        check_vma=False,
    )
```

```python
import functools
import math

import jax
import jax.numpy as jnp
from jax import lax
from jax.experimental import pallas as pl
from jax.experimental.pallas import tpu as pltpu
from jax.sharding import PartitionSpec as P

QUERY_HEADS = 8
KEY_VALUE_HEADS = 2
HEAD_SIZE = 128
GROUP = QUERY_HEADS // KEY_VALUE_HEADS
BLOCKS = 8
SEGMENTS = 4
LANES = 128

NEGATIVE_FILL = -1e30
SCALE = math.log2(math.e) / math.sqrt(HEAD_SIZE)
NT = (((1,), (1,)), ((), ()))


def fused_kernel(
    dest_ref, seg_ref, events_hbm, wq_hbm, wk_hbm, wv_hbm, out_ref,
    events, wq, wk, wv, rows_sorted, info_send, info, kv_send, kv, q_local, q_all, q_pairs,
    pair_pos, pair_start, key_pos, values_t, best, accum, o_send, o_recv,
    load_sem, info_ssem, info_rsem, kv_ssem, kv_rsem, q_sem, o_ssem, o_rsem,
):
    tokens = events.shape[0]
    n = BLOCKS
    blk = tokens // n
    wide = GROUP * HEAD_SIZE
    me = lax.axis_index("ctx")
    core = me % 2
    chip = me // 2
    sibling = chip * 2 + 1 - core
    f32 = jnp.float32

    loads = [
        pltpu.make_async_copy(src, dst, load_sem.at[k])
        for k, (src, dst) in enumerate(
            ((events_hbm, events), (wk_hbm, wk), (wv_hbm, wv), (wq_hbm, wq))
        )
    ]
    for load in loads:
        load.start()

    barrier = pltpu.get_barrier_semaphore()
    for d in range(1, n):
        pl.semaphore_signal(
            barrier, inc=1, device_id={"ctx": (me + d) % n}, device_id_type=pl.DeviceIdType.MESH
        )

    dest = dest_ref[...]
    target = jnp.zeros_like(dest)
    for j in range(1, n):
        target = target + (dest >= j * tokens).astype(jnp.int32)
    row_of = lax.broadcasted_iota(jnp.int32, (n, tokens), 0)
    base = jnp.min(
        jnp.where(jnp.broadcast_to(target, (n, tokens)) == row_of, dest.astype(f32), 1e9),
        axis=1, keepdims=True,
    )
    below = jnp.sum(
        jnp.where(jnp.broadcast_to(seg_ref[...], (n, tokens)) < row_of, 1.0, 0.0),
        axis=1, keepdims=True,
    )
    info_send[0:n, :] = jnp.broadcast_to(base, (n, LANES))
    info_send[n : 2 * n, :] = jnp.broadcast_to(below, (n, LANES))
    info[me] = info_send[...]

    lane = lax.broadcasted_iota(jnp.int32, (1, tokens), 1)
    rank = target * blk + lane % blk
    place = lax.broadcasted_iota(jnp.int32, (tokens, tokens), 0) == rank
    order = jnp.where(place, 1.0, 0.0).astype(jnp.bfloat16)

    pl.semaphore_wait(barrier, n - 1)

    def info_copy(d):
        peer = (me + d) % n
        return pltpu.make_async_remote_copy(
            info_send, info.at[me], info_ssem.at[d], info_rsem.at[me],
            device_id={"ctx": peer}, device_id_type=pl.DeviceIdType.MESH,
        )

    for d in range(1, n):
        info_copy(d).start()

    loads[0].wait()
    rows_sorted[...] = jnp.dot(order, events[...], preferred_element_type=f32).astype(jnp.bfloat16)
    loads[1].wait()
    loads[2].wait()
    keys = jnp.dot(rows_sorted[...], wk[...], preferred_element_type=f32).astype(jnp.bfloat16)
    values = jnp.dot(rows_sorted[...], wv[...], preferred_element_type=f32).astype(jnp.bfloat16)
    for h in range(KEY_VALUE_HEADS):
        cols = slice(h * HEAD_SIZE, (h + 1) * HEAD_SIZE)
        kv_send[h, :, :, 0:HEAD_SIZE] = keys[:, cols].reshape(n, blk, HEAD_SIZE)
        kv_send[h, :, :, HEAD_SIZE:] = values[:, cols].reshape(n, blk, HEAD_SIZE)

    def kv_copy(j, d, c):
        to_chip = (chip + d) % (n // 2)
        return pltpu.make_async_remote_copy(
            kv_send.at[c, j], kv.at[j, me], kv_ssem.at[j, 2 * d + c], kv_rsem.at[j, me],
            device_id={"ctx": to_chip * 2 + c}, device_id_type=pl.DeviceIdType.MESH,
        )

    def sibling_kv(j):
        return pltpu.make_async_remote_copy(
            kv_send.at[1 - core, j], kv.at[j, me], kv_ssem.at[j, 0], kv_rsem.at[j, me],
            device_id={"ctx": sibling}, device_id_type=pl.DeviceIdType.MESH,
        )

    @pl.loop(0, n)
    def _(j):
        for d in range(1, n // 2):
            for c in range(2):
                kv_copy(j, d, c).start()
        sibling_kv(j).start()
        kv[j, me] = kv_send[core, j]

    loads[3].wait()
    for h in range(KEY_VALUE_HEADS):
        query = jnp.dot(
            rows_sorted[...], wq[:, h * wide : (h + 1) * wide], preferred_element_type=f32
        ).astype(jnp.bfloat16)
        for e in range(GROUP):
            q_local[h, :, e] = query[:, e * HEAD_SIZE : (e + 1) * HEAD_SIZE].reshape(
                n, blk, HEAD_SIZE
            )
    q_copy = pltpu.make_async_remote_copy(
        q_local.at[1 - core], q_all.at[core], q_sem.at[0], q_sem.at[1],
        device_id={"ctx": sibling}, device_id_type=pl.DeviceIdType.MESH,
    )
    q_copy.start()
    q_all[core] = q_local[core]

    best[...] = jnp.full(best.shape, NEGATIVE_FILL, f32)
    accum[...] = jnp.zeros(accum.shape, f32)
    values_t[HEAD_SIZE:, :] = jnp.ones((values_t.shape[0] - HEAD_SIZE, tokens), jnp.bfloat16)

    for d in range(1, n):
        source = (me + d) % n
        pltpu.make_async_remote_copy(
            info_send, info.at[source], info_ssem.at[d], info_rsem.at[source],
            device_id={"ctx": source}, device_id_type=pl.DeviceIdType.MESH,
        ).wait_recv()

    counts = jnp.sum(info[:, n : 2 * n, :], axis=0)
    pair = lax.broadcasted_iota(jnp.int32, (n, 2 * blk), 1)
    for c in range(n // 2):
        where = jnp.where(pair < blk, info[2 * c, 0:n, :], info[2 * c + 1, 0:n, :])
        pair_pos[c] = where + (pair % blk).astype(f32)
    mine = pair_pos[chip]
    start = jnp.zeros_like(mine)
    for s in range(1, SEGMENTS):
        edge = jnp.broadcast_to(counts[s : s + 1, :], mine.shape)
        start = jnp.maximum(start, jnp.where(mine >= edge, edge, 0.0))
    pair_start[...] = start

    q_copy.wait_recv()
    for e in range(GROUP):
        for c in range(2):
            first = (2 * e + c) * blk
            q_pairs[:, first : first + blk, :] = q_all[c, :, e]

    def o_copy(i):
        return pltpu.make_async_remote_copy(
            o_send.at[i], o_recv.at[core, chip], o_ssem.at[i], o_rsem.at[me],
            device_id={"ctx": i}, device_id_type=pl.DeviceIdType.MESH,
        )

    @pl.loop(0, n)
    def _(j):
        for d in range(1, n):
            source = (me + d) % n
            pltpu.make_async_remote_copy(
                kv_send.at[0, j], kv.at[j, source], kv_ssem.at[j, 0], kv_rsem.at[j, source],
                device_id={"ctx": source}, device_id_type=pl.DeviceIdType.MESH,
            ).wait_recv()
        block = kv[j].reshape(tokens, 2 * HEAD_SIZE)
        values_t[0:HEAD_SIZE, :] = block[:, HEAD_SIZE:].astype(f32).T.astype(jnp.bfloat16)
        for s in range(n):
            key_pos[s * blk : (s + 1) * blk, :] = info[s, pl.ds(j, 1), :] + lax.broadcasted_iota(
                jnp.int32, (blk, LANES), 0
            ).astype(f32)
        key_tile = block[:, 0:HEAD_SIZE]

        @pl.loop(j, n)
        def _(i):
            here = pair_pos[chip, pl.ds(i, 1), :]
            start = pair_start[pl.ds(i, 1), :]
            at = key_pos[...]
            bias = jnp.where((at >= start) & (at <= here), 0.0, NEGATIVE_FILL)
            bias = jnp.concatenate([bias, bias], axis=1)
            halves = range(2)
            wide_cols = [slice(h * 4 * blk, (h + 1) * 4 * blk) for h in halves]
            old = [best[i, :, cols] for cols in wide_cols]
            held = [accum[i, :, cols] for cols in wide_cols]
            scores = [
                lax.dot_general(
                    key_tile, q_pairs[i, h * 4 * blk : (h + 1) * 4 * blk, :], NT, preferred_element_type=f32
                )
                + bias
                for h in halves
            ]
            fresh = [jnp.maximum(old[h], jnp.max(scores[h], axis=0, keepdims=True)) for h in halves]
            weights = [jnp.exp2((scores[h] - fresh[h]) * SCALE).astype(jnp.bfloat16) for h in halves]
            added = [jnp.dot(values_t[...], weights[h], preferred_element_type=f32) for h in halves]
            for h in halves:
                best[i, :, wide_cols[h]] = fresh[h]
                accum[i, :, wide_cols[h]] = held[h] * jnp.exp2((old[h] - fresh[h]) * SCALE) + added[h]

            @pl.when(i == j)
            def _():
                for e in range(GROUP):
                    cols = slice(e * 2 * blk, (e + 1) * 2 * blk)
                    mixed = accum[i, 0:HEAD_SIZE, cols] / accum[i, HEAD_SIZE : HEAD_SIZE + 1, cols]
                    o_send[i, :, e * HEAD_SIZE : (e + 1) * HEAD_SIZE] = mixed.T.astype(jnp.bfloat16)

                @pl.when(i != me)
                def _():
                    o_copy(i).start()

                @pl.when(i == me)
                def _():
                    o_recv[core, chip] = o_send[i]

    origin = (me * tokens).astype(f32)
    into = jnp.concatenate([pair_pos[c, pl.ds(me, 1), :] for c in range(n // 2)], axis=1) - origin
    row = lax.broadcasted_iota(jnp.int32, (tokens, tokens), 0).astype(f32)
    order = jnp.where(row == into, 1.0, 0.0).astype(jnp.bfloat16)
    for d in range(1, n):
        source = (me + d) % n
        pltpu.make_async_remote_copy(
            o_send.at[0], o_recv.at[source % 2, source // 2], o_ssem.at[0], o_rsem.at[source],
            device_id={"ctx": source}, device_id_type=pl.DeviceIdType.MESH,
        ).wait_recv()
    for c in range(2):
        got = o_recv[c].reshape(tokens, wide)
        out_ref[:, c * wide : (c + 1) * wide] = jnp.dot(
            order, got, preferred_element_type=f32
        ).astype(jnp.bfloat16)

    for d in range(1, n):
        info_copy(d).wait_send()
    q_copy.wait_send()

    @pl.loop(0, n)
    def _(j):
        for d in range(1, n // 2):
            for c in range(2):
                kv_copy(j, d, c).wait_send()
        sibling_kv(j).wait_send()

        @pl.when(j != me)
        def _():
            o_copy(j).wait_send()


def on_device_fused(events, destination, segment, w_query, key_weight, value_weight):
    tokens, width = events.shape
    n = BLOCKS
    blk = tokens // n
    wide = GROUP * HEAD_SIZE
    bf16, f32 = jnp.bfloat16, jnp.float32
    vmem = pl.BlockSpec(memory_space=pltpu.VMEM)
    hbm = pl.BlockSpec(memory_space=pl.ANY)
    dma = pltpu.SemaphoreType.DMA
    return pl.pallas_call(
        fused_kernel,
        out_shape=jax.ShapeDtypeStruct((tokens, QUERY_HEADS * HEAD_SIZE), bf16),
        in_specs=[vmem, vmem, hbm, hbm, hbm, hbm],
        out_specs=vmem,
        scratch_shapes=[
            pltpu.VMEM((tokens, width), bf16),
            pltpu.VMEM(w_query.shape, bf16),
            pltpu.VMEM(key_weight.shape, bf16),
            pltpu.VMEM(value_weight.shape, bf16),
            pltpu.VMEM((tokens, width), bf16),
            pltpu.VMEM((2 * n, LANES), f32),
            pltpu.VMEM((n, 2 * n, LANES), f32),
            pltpu.VMEM((KEY_VALUE_HEADS, n, blk, 2 * HEAD_SIZE), bf16),
            pltpu.VMEM((n, n, blk, 2 * HEAD_SIZE), bf16),
            pltpu.VMEM((KEY_VALUE_HEADS, n, GROUP, blk, HEAD_SIZE), bf16),
            pltpu.VMEM((2, n, GROUP, blk, HEAD_SIZE), bf16),
            pltpu.VMEM((n, GROUP * 2 * blk, HEAD_SIZE), bf16),
            pltpu.VMEM((n // 2, n, LANES), f32),
            pltpu.VMEM((n, LANES), f32),
            pltpu.VMEM((tokens, LANES), f32),
            pltpu.VMEM((HEAD_SIZE + 16, tokens), bf16),
            pltpu.VMEM((n, 1, GROUP * 2 * blk), f32),
            pltpu.VMEM((n, HEAD_SIZE + 16, GROUP * 2 * blk), f32),
            pltpu.VMEM((n, 2 * blk, wide), bf16),
            pltpu.VMEM((2, n // 2, 2 * blk, wide), bf16),
            dma((4,)),
            dma((n,)),
            dma((n,)),
            dma((n, n)),
            dma((n, n)),
            dma((2,)),
            dma((n,)),
            dma((n,)),
        ],
        compiler_params=pltpu.CompilerParams(
            collective_id=0, has_side_effects=True, vmem_limit_bytes=56 * 1024 * 1024
        ),
    )(destination.reshape(1, tokens), segment.reshape(1, tokens), events, w_query, key_weight, value_weight)


def on_device_general(events, destination, segment, w_query, key_weight, value_weight):
    token_count = events.shape[0]
    width = events.shape[1]
    ndevices = lax.axis_size("ctx")
    myself = lax.axis_index("ctx")
    group_size = QUERY_HEADS // KEY_VALUE_HEADS
    score_scale = 1.0 / math.sqrt(HEAD_SIZE)
    lanes = jnp.arange(ndevices, dtype=jnp.int32)
    local_rows = jnp.arange(token_count, dtype=jnp.int32)
    target = destination // token_count
    place = destination % token_count
    bucket = token_count // BLOCKS
    own_position = myself * token_count + local_rows
    onehot = (target[:, None] == lanes[None, :]).astype(jnp.int32)
    earlier = (local_rows[None, :] < local_rows[:, None]).astype(jnp.float32)
    before = jnp.dot(earlier, onehot.astype(jnp.float32)).astype(jnp.int32)
    slot = jnp.sum(before * onehot, axis=1)
    index = target * bucket + slot
    send_rows = (
        jnp.zeros((ndevices * bucket, width), events.dtype)
        .at[index]
        .set(events)
        .reshape(ndevices, bucket, width)
    )
    send_place = (
        jnp.full((ndevices * bucket,), token_count, jnp.int32)
        .at[index]
        .set(place)
        .reshape(ndevices, bucket)
    )
    got_rows, got_place = (
        lax.all_to_all(send_rows, "ctx", split_axis=0, concat_axis=0, tiled=True),
        lax.all_to_all(send_place, "ctx", split_axis=0, concat_axis=0, tiled=True),
    )
    packed = (
        jnp.zeros((token_count, width), events.dtype)
        .at[got_place.reshape(-1)]
        .set(got_rows.reshape(-1, width), mode="drop")
    )
    query_rows = jnp.dot(packed, w_query, preferred_element_type=jnp.float32).astype(jnp.bfloat16)
    key_rows = jnp.dot(packed, key_weight, preferred_element_type=jnp.float32).astype(jnp.bfloat16)
    value_rows = jnp.dot(packed, value_weight, preferred_element_type=jnp.float32).astype(
        jnp.bfloat16
    )
    query_head_rows = query_rows.reshape(token_count, KEY_VALUE_HEADS, group_size, HEAD_SIZE)
    query_seg = segment.astype(jnp.float32)
    seg_sent = segment.astype(jnp.bfloat16)
    start_state = (
        jnp.full((KEY_VALUE_HEADS, group_size, token_count), NEGATIVE_FILL, jnp.float32),
        jnp.zeros((KEY_VALUE_HEADS, group_size, token_count), jnp.float32),
        jnp.zeros((KEY_VALUE_HEADS, group_size, token_count, HEAD_SIZE), jnp.float32),
    )
    carry = start_state
    key_portion = lax.all_gather(key_rows, "ctx", axis=0, tiled=True)
    value_portion = lax.all_gather(value_rows, "ctx", axis=0, tiled=True)
    seg_piece = lax.all_gather(seg_sent, "ctx", axis=0, tiled=True)
    token_rows = key_portion.shape[0]
    block_step = 512
    event_count = token_rows // block_step
    key_block_list = key_portion.reshape(event_count, block_step, KEY_VALUE_HEADS, HEAD_SIZE)
    value_block_list = value_portion.reshape(event_count, block_step, KEY_VALUE_HEADS, HEAD_SIZE)
    seg_blocks = seg_piece.astype(jnp.float32).reshape(event_count, block_step)
    offsets = jnp.arange(event_count, dtype=jnp.int32) * block_step

    def one_block(state, inputs):
        key_tile_rows, value_block, seg_block, offset = inputs
        key_pos = offset + jnp.arange(block_step, dtype=jnp.int32)
        allowed = (seg_block[None, :] == query_seg[:, None]) & (
            key_pos[None, :] <= own_position[:, None]
        )
        best, total_tokens, accum = state
        logit_scores = (
            jnp.einsum(
                "qxli,oxi->xlqo", query_head_rows, key_tile_rows, preferred_element_type=jnp.float32
            )
            * score_scale
        )
        logit_scores = jnp.where(allowed, logit_scores, NEGATIVE_FILL)
        fresh = jnp.maximum(best, jnp.max(logit_scores, axis=-1))
        softmax_weights = jnp.where(allowed, jnp.exp(logit_scores - fresh[..., None]), 0.0)
        shrink = jnp.exp(best - fresh)
        total_tokens = total_tokens * shrink + jnp.sum(softmax_weights, axis=-1)
        accum = accum * shrink[..., None] + jnp.einsum(
            "qlwc,cqh->qlwh",
            softmax_weights.astype(jnp.bfloat16),
            value_block,
            preferred_element_type=jnp.float32,
        )
        state = (fresh, total_tokens, accum)
        return (state, None)

    carry, _ = lax.scan(one_block, carry, (key_block_list, value_block_list, seg_blocks, offsets))
    best, total_tokens, accum = carry
    result = (
        (accum / total_tokens[..., None])
        .transpose(2, 0, 1, 3)
        .reshape(token_count, QUERY_HEADS * HEAD_SIZE)
        .astype(jnp.bfloat16)
    )
    return result


def solution(mesh):
    def on_device(events, *rest):
        fits = mesh.shape["ctx"] == BLOCKS and events.shape[0] == BLOCKS * LANES // 2
        return (on_device_fused if fits else on_device_general)(events, *rest)

    return jax.shard_map(
        on_device,
        mesh=mesh,
        in_specs=(P(("dp", "ctx"), None), P(("dp", "ctx")), P(("dp", "ctx")), P(), P(), P()),
        out_specs=P(("dp", "ctx"), None),
        check_vma=False,
    )
```

```python
import functools
import math

import jax
import jax.numpy as jnp
from jax import lax
from jax.experimental import pallas as pl
from jax.experimental.pallas import tpu as pltpu
from jax.sharding import PartitionSpec as P

QUERY_HEADS = 8
KEY_VALUE_HEADS = 2
HEAD_SIZE = 128
GROUP = QUERY_HEADS // KEY_VALUE_HEADS
BLOCKS = 8
SEGMENTS = 4
LANES = 128

NEGATIVE_FILL = -1e30
SCALE = math.log2(math.e) / math.sqrt(HEAD_SIZE)
NT = (((1,), (1,)), ((), ()))


def fused_kernel(
    dest_ref, seg_ref, events_hbm, wq_hbm, wk_hbm, wv_hbm, out_ref,
    events, wq, wk, wv, rows_sorted, info_send, info, kv_send, kv, q_local, q_all, q_pairs,
    pair_pos, pair_start, key_pos, values_t, best, accum, o_send, o_recv,
    load_sem, info_ssem, info_rsem, kv_ssem, kv_rsem, q_sem, o_ssem, o_rsem,
):
    tokens = events.shape[0]
    n = BLOCKS
    blk = tokens // n
    wide = GROUP * HEAD_SIZE
    me = lax.axis_index("ctx")
    core = me % 2
    chip = me // 2
    sibling = chip * 2 + 1 - core
    f32 = jnp.float32

    loads = [
        pltpu.make_async_copy(src, dst, load_sem.at[k])
        for k, (src, dst) in enumerate(
            ((events_hbm, events), (wk_hbm, wk), (wv_hbm, wv), (wq_hbm, wq))
        )
    ]
    for load in loads:
        load.start()

    barrier = pltpu.get_barrier_semaphore()
    for d in range(1, n):
        pl.semaphore_signal(
            barrier, inc=1, device_id={"ctx": (me + d) % n}, device_id_type=pl.DeviceIdType.MESH
        )

    dest = dest_ref[...]
    target = jnp.zeros_like(dest)
    for j in range(1, n):
        target = target + (dest >= j * tokens).astype(jnp.int32)
    row_of = lax.broadcasted_iota(jnp.int32, (n, tokens), 0)
    base = jnp.min(
        jnp.where(jnp.broadcast_to(target, (n, tokens)) == row_of, dest.astype(f32), 1e9),
        axis=1, keepdims=True,
    )
    below = jnp.sum(
        jnp.where(jnp.broadcast_to(seg_ref[...], (n, tokens)) < row_of, 1.0, 0.0),
        axis=1, keepdims=True,
    )
    info_send[0:n, :] = jnp.broadcast_to(base, (n, LANES))
    info_send[n : 2 * n, :] = jnp.broadcast_to(below, (n, LANES))
    info[me] = info_send[...]

    lane = lax.broadcasted_iota(jnp.int32, (1, tokens), 1)
    rank = target * blk + lane % blk
    place = lax.broadcasted_iota(jnp.int32, (tokens, tokens), 0) == rank
    order = jnp.where(place, 1.0, 0.0).astype(jnp.bfloat16)

    pl.semaphore_wait(barrier, n - 1)

    def info_copy(d):
        peer = (me + d) % n
        return pltpu.make_async_remote_copy(
            info_send, info.at[me], info_ssem.at[d], info_rsem.at[me],
            device_id={"ctx": peer}, device_id_type=pl.DeviceIdType.MESH,
        )

    for d in range(1, n):
        info_copy(d).start()

    loads[0].wait()
    def kv_copy(j, d, c):
        to_chip = (chip + d) % (n // 2)
        return pltpu.make_async_remote_copy(
            kv_send.at[c, j], kv.at[j, me], kv_ssem.at[j, 2 * d + c], kv_rsem.at[j, me],
            device_id={"ctx": to_chip * 2 + c}, device_id_type=pl.DeviceIdType.MESH,
        )

    def sibling_kv(j):
        return pltpu.make_async_remote_copy(
            kv_send.at[1 - core, j], kv.at[j, me], kv_ssem.at[j, 0], kv_rsem.at[j, me],
            device_id={"ctx": sibling}, device_id_type=pl.DeviceIdType.MESH,
        )

    part = 2 * blk
    loads[1].wait()
    loads[2].wait()
    for p in range(n // 2):
        here = slice(p * part, (p + 1) * part)
        rows = jnp.dot(order[here], events[...], preferred_element_type=f32).astype(jnp.bfloat16)
        rows_sorted[here, :] = rows
        keys = jnp.dot(rows, wk[...], preferred_element_type=f32).astype(jnp.bfloat16)
        values = jnp.dot(rows, wv[...], preferred_element_type=f32).astype(jnp.bfloat16)
        for h in range(KEY_VALUE_HEADS):
            cols = slice(h * HEAD_SIZE, (h + 1) * HEAD_SIZE)
            kv_send[h, 2 * p : 2 * p + 2, :, 0:HEAD_SIZE] = keys[:, cols].reshape(2, blk, HEAD_SIZE)
            kv_send[h, 2 * p : 2 * p + 2, :, HEAD_SIZE:] = values[:, cols].reshape(2, blk, HEAD_SIZE)
        for j in (2 * p, 2 * p + 1):
            for d in range(1, n // 2):
                for c in range(2):
                    kv_copy(j, d, c).start()
            sibling_kv(j).start()
            kv[j, me] = kv_send[core, j]

    loads[3].wait()
    for h in range(KEY_VALUE_HEADS):
        query = jnp.dot(
            rows_sorted[...], wq[:, h * wide : (h + 1) * wide], preferred_element_type=f32
        ).astype(jnp.bfloat16)
        for e in range(GROUP):
            q_local[h, :, e] = query[:, e * HEAD_SIZE : (e + 1) * HEAD_SIZE].reshape(
                n, blk, HEAD_SIZE
            )
    q_copy = pltpu.make_async_remote_copy(
        q_local.at[1 - core], q_all.at[core], q_sem.at[0], q_sem.at[1],
        device_id={"ctx": sibling}, device_id_type=pl.DeviceIdType.MESH,
    )
    q_copy.start()
    q_all[core] = q_local[core]

    best[...] = jnp.full(best.shape, NEGATIVE_FILL, f32)
    accum[...] = jnp.zeros(accum.shape, f32)
    values_t[HEAD_SIZE:, :] = jnp.ones((values_t.shape[0] - HEAD_SIZE, tokens), jnp.bfloat16)

    for d in range(1, n):
        source = (me + d) % n
        pltpu.make_async_remote_copy(
            info_send, info.at[source], info_ssem.at[d], info_rsem.at[source],
            device_id={"ctx": source}, device_id_type=pl.DeviceIdType.MESH,
        ).wait_recv()

    counts = jnp.sum(info[:, n : 2 * n, :], axis=0)
    pair = lax.broadcasted_iota(jnp.int32, (n, 2 * blk), 1)
    for c in range(n // 2):
        where = jnp.where(pair < blk, info[2 * c, 0:n, :], info[2 * c + 1, 0:n, :])
        pair_pos[c] = where + (pair % blk).astype(f32)
    mine = pair_pos[chip]
    start = jnp.zeros_like(mine)
    for s in range(1, SEGMENTS):
        edge = jnp.broadcast_to(counts[s : s + 1, :], mine.shape)
        start = jnp.maximum(start, jnp.where(mine >= edge, edge, 0.0))
    pair_start[...] = start

    q_copy.wait_recv()
    for e in range(GROUP):
        for c in range(2):
            first = (2 * e + c) * blk
            q_pairs[:, first : first + blk, :] = q_all[c, :, e]

    def o_copy(i):
        return pltpu.make_async_remote_copy(
            o_send.at[i], o_recv.at[core, chip], o_ssem.at[i], o_rsem.at[me],
            device_id={"ctx": i}, device_id_type=pl.DeviceIdType.MESH,
        )

    @pl.loop(0, n)
    def _(j):
        for d in range(1, n):
            source = (me + d) % n
            pltpu.make_async_remote_copy(
                kv_send.at[0, j], kv.at[j, source], kv_ssem.at[j, 0], kv_rsem.at[j, source],
                device_id={"ctx": source}, device_id_type=pl.DeviceIdType.MESH,
            ).wait_recv()
        block = kv[j].reshape(tokens, 2 * HEAD_SIZE)
        values_t[0:HEAD_SIZE, :] = block[:, HEAD_SIZE:].astype(f32).T.astype(jnp.bfloat16)
        for s in range(n):
            key_pos[s * blk : (s + 1) * blk, :] = info[s, pl.ds(j, 1), :] + lax.broadcasted_iota(
                jnp.int32, (blk, LANES), 0
            ).astype(f32)
        key_tile = block[:, 0:HEAD_SIZE]

        @pl.loop(j, n)
        def _(i):
            here = pair_pos[chip, pl.ds(i, 1), :]
            start = pair_start[pl.ds(i, 1), :]
            at = key_pos[...]
            bias = jnp.where((at >= start) & (at <= here), 0.0, NEGATIVE_FILL)
            bias = jnp.concatenate([bias, bias], axis=1)
            halves = range(2)
            wide_cols = [slice(h * 4 * blk, (h + 1) * 4 * blk) for h in halves]
            old = [best[i, :, cols] for cols in wide_cols]
            held = [accum[i, :, cols] for cols in wide_cols]
            scores = [
                lax.dot_general(
                    key_tile, q_pairs[i, h * 4 * blk : (h + 1) * 4 * blk, :], NT, preferred_element_type=f32
                )
                + bias
                for h in halves
            ]
            fresh = [jnp.maximum(old[h], jnp.max(scores[h], axis=0, keepdims=True)) for h in halves]
            weights = [jnp.exp2((scores[h] - fresh[h]) * SCALE).astype(jnp.bfloat16) for h in halves]
            added = [jnp.dot(values_t[...], weights[h], preferred_element_type=f32) for h in halves]
            for h in halves:
                best[i, :, wide_cols[h]] = fresh[h]
                accum[i, :, wide_cols[h]] = held[h] * jnp.exp2((old[h] - fresh[h]) * SCALE) + added[h]

            @pl.when(i == j)
            def _():
                for e in range(GROUP):
                    cols = slice(e * 2 * blk, (e + 1) * 2 * blk)
                    mixed = accum[i, 0:HEAD_SIZE, cols] / accum[i, HEAD_SIZE : HEAD_SIZE + 1, cols]
                    o_send[i, :, e * HEAD_SIZE : (e + 1) * HEAD_SIZE] = mixed.T.astype(jnp.bfloat16)

                @pl.when(i != me)
                def _():
                    o_copy(i).start()

                @pl.when(i == me)
                def _():
                    o_recv[core, chip] = o_send[i]

    origin = (me * tokens).astype(f32)
    into = jnp.concatenate([pair_pos[c, pl.ds(me, 1), :] for c in range(n // 2)], axis=1) - origin
    row = lax.broadcasted_iota(jnp.int32, (tokens, tokens), 0).astype(f32)
    order = jnp.where(row == into, 1.0, 0.0).astype(jnp.bfloat16)
    for d in range(1, n):
        source = (me + d) % n
        pltpu.make_async_remote_copy(
            o_send.at[0], o_recv.at[source % 2, source // 2], o_ssem.at[0], o_rsem.at[source],
            device_id={"ctx": source}, device_id_type=pl.DeviceIdType.MESH,
        ).wait_recv()
    for c in range(2):
        got = o_recv[c].reshape(tokens, wide)
        out_ref[:, c * wide : (c + 1) * wide] = jnp.dot(
            order, got, preferred_element_type=f32
        ).astype(jnp.bfloat16)

    for d in range(1, n):
        info_copy(d).wait_send()
    q_copy.wait_send()

    @pl.loop(0, n)
    def _(j):
        for d in range(1, n // 2):
            for c in range(2):
                kv_copy(j, d, c).wait_send()
        sibling_kv(j).wait_send()

        @pl.when(j != me)
        def _():
            o_copy(j).wait_send()


def on_device_fused(events, destination, segment, w_query, key_weight, value_weight):
    tokens, width = events.shape
    n = BLOCKS
    blk = tokens // n
    wide = GROUP * HEAD_SIZE
    bf16, f32 = jnp.bfloat16, jnp.float32
    vmem = pl.BlockSpec(memory_space=pltpu.VMEM)
    hbm = pl.BlockSpec(memory_space=pl.ANY)
    dma = pltpu.SemaphoreType.DMA
    return pl.pallas_call(
        fused_kernel,
        out_shape=jax.ShapeDtypeStruct((tokens, QUERY_HEADS * HEAD_SIZE), bf16),
        in_specs=[vmem, vmem, hbm, hbm, hbm, hbm],
        out_specs=vmem,
        scratch_shapes=[
            pltpu.VMEM((tokens, width), bf16),
            pltpu.VMEM(w_query.shape, bf16),
            pltpu.VMEM(key_weight.shape, bf16),
            pltpu.VMEM(value_weight.shape, bf16),
            pltpu.VMEM((tokens, width), bf16),
            pltpu.VMEM((2 * n, LANES), f32),
            pltpu.VMEM((n, 2 * n, LANES), f32),
            pltpu.VMEM((KEY_VALUE_HEADS, n, blk, 2 * HEAD_SIZE), bf16),
            pltpu.VMEM((n, n, blk, 2 * HEAD_SIZE), bf16),
            pltpu.VMEM((KEY_VALUE_HEADS, n, GROUP, blk, HEAD_SIZE), bf16),
            pltpu.VMEM((2, n, GROUP, blk, HEAD_SIZE), bf16),
            pltpu.VMEM((n, GROUP * 2 * blk, HEAD_SIZE), bf16),
            pltpu.VMEM((n // 2, n, LANES), f32),
            pltpu.VMEM((n, LANES), f32),
            pltpu.VMEM((tokens, LANES), f32),
            pltpu.VMEM((HEAD_SIZE + 16, tokens), bf16),
            pltpu.VMEM((n, 1, GROUP * 2 * blk), f32),
            pltpu.VMEM((n, HEAD_SIZE + 16, GROUP * 2 * blk), f32),
            pltpu.VMEM((n, 2 * blk, wide), bf16),
            pltpu.VMEM((2, n // 2, 2 * blk, wide), bf16),
            dma((4,)),
            dma((n,)),
            dma((n,)),
            dma((n, n)),
            dma((n, n)),
            dma((2,)),
            dma((n,)),
            dma((n,)),
        ],
        compiler_params=pltpu.CompilerParams(
            collective_id=0, has_side_effects=True, vmem_limit_bytes=56 * 1024 * 1024
        ),
    )(destination.reshape(1, tokens), segment.reshape(1, tokens), events, w_query, key_weight, value_weight)


def on_device_general(events, destination, segment, w_query, key_weight, value_weight):
    token_count = events.shape[0]
    width = events.shape[1]
    ndevices = lax.axis_size("ctx")
    myself = lax.axis_index("ctx")
    group_size = QUERY_HEADS // KEY_VALUE_HEADS
    score_scale = 1.0 / math.sqrt(HEAD_SIZE)
    lanes = jnp.arange(ndevices, dtype=jnp.int32)
    local_rows = jnp.arange(token_count, dtype=jnp.int32)
    target = destination // token_count
    place = destination % token_count
    bucket = token_count // BLOCKS
    own_position = myself * token_count + local_rows
    onehot = (target[:, None] == lanes[None, :]).astype(jnp.int32)
    earlier = (local_rows[None, :] < local_rows[:, None]).astype(jnp.float32)
    before = jnp.dot(earlier, onehot.astype(jnp.float32)).astype(jnp.int32)
    slot = jnp.sum(before * onehot, axis=1)
    index = target * bucket + slot
    send_rows = (
        jnp.zeros((ndevices * bucket, width), events.dtype)
        .at[index]
        .set(events)
        .reshape(ndevices, bucket, width)
    )
    send_place = (
        jnp.full((ndevices * bucket,), token_count, jnp.int32)
        .at[index]
        .set(place)
        .reshape(ndevices, bucket)
    )
    got_rows, got_place = (
        lax.all_to_all(send_rows, "ctx", split_axis=0, concat_axis=0, tiled=True),
        lax.all_to_all(send_place, "ctx", split_axis=0, concat_axis=0, tiled=True),
    )
    packed = (
        jnp.zeros((token_count, width), events.dtype)
        .at[got_place.reshape(-1)]
        .set(got_rows.reshape(-1, width), mode="drop")
    )
    query_rows = jnp.dot(packed, w_query, preferred_element_type=jnp.float32).astype(jnp.bfloat16)
    key_rows = jnp.dot(packed, key_weight, preferred_element_type=jnp.float32).astype(jnp.bfloat16)
    value_rows = jnp.dot(packed, value_weight, preferred_element_type=jnp.float32).astype(
        jnp.bfloat16
    )
    query_head_rows = query_rows.reshape(token_count, KEY_VALUE_HEADS, group_size, HEAD_SIZE)
    query_seg = segment.astype(jnp.float32)
    seg_sent = segment.astype(jnp.bfloat16)
    start_state = (
        jnp.full((KEY_VALUE_HEADS, group_size, token_count), NEGATIVE_FILL, jnp.float32),
        jnp.zeros((KEY_VALUE_HEADS, group_size, token_count), jnp.float32),
        jnp.zeros((KEY_VALUE_HEADS, group_size, token_count, HEAD_SIZE), jnp.float32),
    )
    carry = start_state
    key_portion = lax.all_gather(key_rows, "ctx", axis=0, tiled=True)
    value_portion = lax.all_gather(value_rows, "ctx", axis=0, tiled=True)
    seg_piece = lax.all_gather(seg_sent, "ctx", axis=0, tiled=True)
    token_rows = key_portion.shape[0]
    block_step = 512
    event_count = token_rows // block_step
    key_block_list = key_portion.reshape(event_count, block_step, KEY_VALUE_HEADS, HEAD_SIZE)
    value_block_list = value_portion.reshape(event_count, block_step, KEY_VALUE_HEADS, HEAD_SIZE)
    seg_blocks = seg_piece.astype(jnp.float32).reshape(event_count, block_step)
    offsets = jnp.arange(event_count, dtype=jnp.int32) * block_step

    def one_block(state, inputs):
        key_tile_rows, value_block, seg_block, offset = inputs
        key_pos = offset + jnp.arange(block_step, dtype=jnp.int32)
        allowed = (seg_block[None, :] == query_seg[:, None]) & (
            key_pos[None, :] <= own_position[:, None]
        )
        best, total_tokens, accum = state
        logit_scores = (
            jnp.einsum(
                "qxli,oxi->xlqo", query_head_rows, key_tile_rows, preferred_element_type=jnp.float32
            )
            * score_scale
        )
        logit_scores = jnp.where(allowed, logit_scores, NEGATIVE_FILL)
        fresh = jnp.maximum(best, jnp.max(logit_scores, axis=-1))
        softmax_weights = jnp.where(allowed, jnp.exp(logit_scores - fresh[..., None]), 0.0)
        shrink = jnp.exp(best - fresh)
        total_tokens = total_tokens * shrink + jnp.sum(softmax_weights, axis=-1)
        accum = accum * shrink[..., None] + jnp.einsum(
            "qlwc,cqh->qlwh",
            softmax_weights.astype(jnp.bfloat16),
            value_block,
            preferred_element_type=jnp.float32,
        )
        state = (fresh, total_tokens, accum)
        return (state, None)

    carry, _ = lax.scan(one_block, carry, (key_block_list, value_block_list, seg_blocks, offsets))
    best, total_tokens, accum = carry
    result = (
        (accum / total_tokens[..., None])
        .transpose(2, 0, 1, 3)
        .reshape(token_count, QUERY_HEADS * HEAD_SIZE)
        .astype(jnp.bfloat16)
    )
    return result


def solution(mesh):
    def on_device(events, *rest):
        fits = mesh.shape["ctx"] == BLOCKS and events.shape[0] == BLOCKS * LANES // 2
        return (on_device_fused if fits else on_device_general)(events, *rest)

    return jax.shard_map(
        on_device,
        mesh=mesh,
        in_specs=(P(("dp", "ctx"), None), P(("dp", "ctx")), P(("dp", "ctx")), P(), P(), P()),
        out_specs=P(("dp", "ctx"), None),
        check_vma=False,
    )
```
